32 devices in a mesh: row: 8 (over z, core), col: 4 (over y, x).
Axes of the slice: x: 2, y: 2, z: 4, core: 2. Of those that a mesh axis runs over, the one named last changes fastest.
Arguments:
- cost_tiles: float32 [8, 4, 64, 128, 128], P('row', 'col'), may hold values from 0 to 66
- tile_rows: int32 [8, 4, 64], P('row', 'col'), may hold values from 0 to 127, as said below
- tile_cols: int32 [8, 4, 64], P('row', 'col'), may hold values from 0 to 127
- tile_count: int32 [8, 4], P('row', 'col'), may hold values from 32 to 64, as said below
- source_logmass: float32 [131072], P('row'), may hold values from -3 to 0
- target_logmass: float32 [65536], P('col'), may hold values from -103 to -100
- target_init: float32 [65536], P('col'), may hold values from -2 to 14
Outputs:
- source_potential: float32 [131072], P('row')
- target_potential: float32 [65536], P('col')
The draws below stay inside these ranges and needn't reach their ends.
Inputs may be any that keep to these rules, and one draw needn't show every extreme that they name: Among the first tile_count slots of a device all (tile_rows, tile_cols) pairs differ; every source block of a row shard appears in such a slot of some device of that shard, and every target block of a col shard likewise. Slots at tile_count or later hold pairs to be ignored. `tile_count`: some device has all 64 slots in use in every draw.
All inputs are finite; a program needn't handle non-finite values.
Results may differ from the reference program's by a relative error of at most 0.00019.
Values sent between devices are 32-bit elements; how exact they have to be, the bound alone decides.
A program may use at most 64 MiB of HBM per device.

```python
import jax
import jax.numpy as jnp
from jax import lax

BLOCK = 128
RB = 128
CB = 128
CAP = 64
ITERS = 2
NSRC = 131072
NTGT = 65536
N_ROW = 8
N_COL = 4


def tile_lists(key):
    base = jax.random.fold_in(key, 7)
    ndev = N_ROW * N_COL
    shard_r = jnp.arange(ndev) // N_COL
    shard_c = jnp.arange(ndev) % N_COL
    cover_r = RB // N_COL
    cover_c = CB // N_ROW
    cover = max(cover_r, cover_c)
    keys = jax.random.split(jax.random.fold_in(base, 1), ndev)
    ranks = jax.vmap(lambda single: jax.random.permutation(single, RB * CB))(keys).astype(jnp.int32)
    steps = jnp.arange(cover)
    forced = (shard_c[:, None] * cover_r + steps[None, :] % cover_r) * CB + shard_r[:, None] * cover_c + steps[None, :] % cover_c
    lanes = jnp.arange(ndev)[:, None] + jnp.zeros((1, cover), jnp.int32)
    ranks = ranks.at[lanes, forced].set(steps[None, :] - cover)
    order = jnp.argsort(ranks, axis=1, stable=True)[:, :CAP].astype(jnp.int32)
    rows = (order // CB).reshape(N_ROW, N_COL, CAP)
    cols = (order % CB).reshape(N_ROW, N_COL, CAP)
    lowest = max(cover, CAP // 4)
    span = CAP - lowest
    first = jax.random.randint(jax.random.fold_in(base, 2), (ndev,), 0, span + 1)
    second = jax.random.randint(jax.random.fold_in(base, 3), (ndev,), 0, span + 1)
    counts = lowest + first * second // max(span, 1)
    busiest = jax.random.randint(jax.random.fold_in(base, 4), (), 0, ndev)
    counts = counts.at[busiest].set(CAP).astype(jnp.int32)
    return (rows, cols, counts.reshape(N_ROW, N_COL))


def draw_tile_rows(key, part):
    return tile_lists(key)[0]


def draw_tile_cols(key, part):
    return tile_lists(key)[1]


def draw_tile_count(key, part):
    return tile_lists(key)[2]


def draw_cost_tiles(key, part):
    shape = (N_ROW, N_COL, CAP, BLOCK, BLOCK)
    rows, cols, counts = tile_lists(key)
    first = jax.random.fold_in(key, 11)
    row_lift = jax.random.uniform(jax.random.fold_in(key, 13), (NSRC,), jnp.float32, 0.0, 30.0)
    col_lift = jax.random.uniform(jax.random.fold_in(key, 14), (NTGT,), jnp.float32, 0.0, 30.0)
    shard_r = jnp.arange(N_ROW).reshape(N_ROW, 1, 1, 1)
    shard_c = jnp.arange(N_COL).reshape(1, N_COL, 1, 1)
    lanes = jnp.arange(BLOCK).reshape(1, 1, 1, BLOCK)
    source_index = ((shard_r * RB + rows[..., None]) * BLOCK + lanes).astype(jnp.int32)
    target_index = ((shard_c * CB + cols[..., None]) * BLOCK + lanes).astype(jnp.int32)
    base = jax.random.uniform(first, shape, jnp.float32, 0.0, 6.0)
    return base + row_lift[source_index][..., :, None] + col_lift[target_index][..., None, :]


def draw_target_init(key, part):
    first = jax.random.fold_in(key, 21)
    drawn = jax.random.uniform(first, (NTGT,), jnp.float32, -2.0, 2.0)
    return drawn


def shard_levels(key, shape, shards, smallest, high):
    factor_of, own = 1.0, jax.random.fold_in(key, 6)
    for position, blocks in shards:
        steps = jnp.exp(jax.random.uniform(jax.random.fold_in(own, position), (blocks,), jnp.float32, smallest / len(shards), high / len(shards)))
        factor_of = factor_of * jnp.repeat(steps, shape[position] // blocks).reshape([-1 if axis == position else 1 for axis in range(len(shape))])
    return factor_of


def setup_inputs(seed: int = 0) -> dict:
    seeds = jax.random.split(jax.random.key(seed), 8)
    cost_tiles = draw_cost_tiles(jax.random.fold_in(seeds[7], 71), 0)
    tile_rows = draw_tile_rows(jax.random.fold_in(seeds[7], 71), 0)
    tile_cols = draw_tile_cols(jax.random.fold_in(seeds[7], 71), 0)
    tile_count = draw_tile_count(jax.random.fold_in(seeds[7], 71), 0)
    source_logmass = jnp.clip(-3.0 + 3.0 * jax.random.uniform(seeds[4], (NSRC,), jnp.float32) ** shard_levels(seeds[4], (NSRC,), ((0, 8),), -0.2, 0.2), -3.0, 0.0)
    target_logmass = jnp.clip(-103.0 + 3.0 * jax.random.uniform(seeds[5], (NTGT,), jnp.float32) ** shard_levels(seeds[5], (NTGT,), ((0, 4),), -0.2, 0.2), -103.0, -100.0)
    target_init = draw_target_init(jax.random.fold_in(seeds[7], 71), 0)
    return {"cost_tiles": cost_tiles, "tile_rows": tile_rows, "tile_cols": tile_cols, "tile_count": tile_count, "source_logmass": source_logmass, "target_logmass": target_logmass, "target_init": target_init}


EPS = 0.1


def side_lse(cost, pot, gather_ids, seg_ids, valid, nseg, rows_side):
    blocks = pot.reshape(-1, BLOCK)
    red = 2 if rows_side else 1

    def scores(tiles, gid):
        part = blocks[gid]
        if rows_side:
            return (part[:, None, :] - tiles) / EPS
        return (part[:, :, None] - tiles) / EPS

    def peak(args):
        tiles, gid = args
        return jnp.max(scores(tiles, gid), axis=red)

    tmax = lax.map(peak, (cost, gather_ids))
    tmax = jnp.where(valid[:, :, None], tmax, -jnp.inf)
    ids = jnp.where(valid, seg_ids, 0).reshape(-1).astype(jnp.int32)
    top = jax.ops.segment_max(tmax.reshape(-1, BLOCK), ids, num_segments=nseg)

    def total(args):
        tiles, gid, sid, okay = args
        shift = top[sid]
        shift = jnp.where(okay[:, None], shift, 0.0)
        if rows_side:
            expo = jnp.exp(scores(tiles, gid) - shift[:, :, None])
        else:
            expo = jnp.exp(scores(tiles, gid) - shift[:, None, :])
        return jnp.where(okay[:, None], jnp.sum(expo, axis=red), 0.0)

    sums = lax.map(total, (cost, gather_ids, seg_ids, valid))
    mass = jax.ops.segment_sum(sums.reshape(-1, BLOCK), ids, num_segments=nseg)
    return (top + jnp.log(mass)).reshape(-1)


def reference(cost_tiles, tile_rows, tile_cols, tile_count, source_logmass, target_logmass, target_init):
    ndev = N_ROW * N_COL
    cost = cost_tiles.reshape(ndev, CAP, BLOCK, BLOCK)
    shard_r = (jnp.arange(ndev) // N_COL).astype(jnp.int32)
    shard_c = (jnp.arange(ndev) % N_COL).astype(jnp.int32)
    grow = (tile_rows.reshape(ndev, CAP) + shard_r[:, None] * RB).astype(jnp.int32)
    gcol = (tile_cols.reshape(ndev, CAP) + shard_c[:, None] * CB).astype(jnp.int32)
    valid = jnp.arange(CAP)[None, :] < tile_count.reshape(-1)[:, None]
    target_potential = target_init
    source_potential = source_logmass
    for step in range(ITERS):
        source_potential = EPS * source_logmass - EPS * side_lse(cost, target_potential, gcol, grow, valid, N_ROW * RB, True)
        target_potential = EPS * target_logmass - EPS * side_lse(cost, source_potential, grow, gcol, valid, N_COL * CB, False)
    return source_potential, target_potential
```

```python
import functools
import math

import jax
import jax.numpy as jnp
from jax import lax
from jax.experimental import pallas as pl
from jax.experimental.pallas import tpu as pltpu
from jax.sharding import PartitionSpec as P

ITERS = 2
EPS = 0.1
LOG2E = math.log2(math.e)
SCALE = LOG2E / EPS
GROUP = 8
LANES = 128
MESH = pl.DeviceIdType.MESH


def split_bf16(x, parts):
    out = []
    for _ in range(parts):
        head = x.astype(jnp.bfloat16)
        out.append(head)
        x = x - head.astype(jnp.float32)
    return out


def kernel(
    cost, rows, cols, count, slog, tlog, tinit,
    s_out, t_out,
    cbuf, lbuf, gbuf, init_pot, seg_s, seg_t, hot_s, hot_t, rep_s, rep_t,
    part_s0, part_s1, part_t0, part_t1,
    mid_s0, mid_s1, mid_t0, mid_t1,
    pot_s0, pot_s1, pot_t0, pot_t1,
    cost_sem, scatter_send_s, scatter_recv_s, gather_send_s, gather_recv_s,
    scatter_send_t, scatter_recv_t, gather_send_t, gather_recv_t,
    *, n_row, n_col,
):
    cap = cbuf.shape[0]
    me = {"row": lax.axis_index("row"), "col": lax.axis_index("col")}
    sizes = {"row": n_row, "col": n_col}

    def peer(axis, o):
        return lax.rem(me[axis] + o, sizes[axis])

    barrier = pltpu.get_barrier_semaphore()
    for axis in ("col", "row"):
        for o in range(1, sizes[axis]):
            pl.semaphore_signal(
                barrier, inc=1, device_id={axis: peer(axis, o)}, device_id_type=MESH
            )

    groups = cap // GROUP

    def fetch(g):
        span = pl.ds(g * GROUP, GROUP)
        return pltpu.make_async_copy(cost.at[0, 0, span], cbuf.at[span], cost_sem.at[g])

    for g in range(groups):
        fetch(g).start()

    total = count[0, 0]
    lane = lax.broadcasted_iota(jnp.int32, (LANES, LANES), 1)
    sub8 = lax.broadcasted_iota(jnp.int32, (GROUP, LANES), 0)
    slot = lax.broadcasted_iota(jnp.int32, (cap, LANES), 0)

    def segment(ids, s):
        return jnp.where(s < total, ids[0, 0, s], -1)

    def prepare(ids, seg, hot, rep):
        nb = hot.shape[0]

        def fill(g, _):
            value = jnp.zeros((GROUP, LANES), jnp.int32)
            for k in range(GROUP):
                value = jnp.where(sub8 == k, segment(ids, g * GROUP + k), value)
            seg[pl.ds(pl.multiple_of(g * GROUP, GROUP), GROUP), :] = value
            return 0

        lax.fori_loop(0, groups, fill, 0)
        mine = seg[...]

        def earlier(g, dup):
            for k in range(GROUP):
                t = g * GROUP + k
                same = (mine == segment(ids, t)) & (slot > t)
                dup = jnp.where(same, 1.0, dup)
            return dup

        dup = lax.fori_loop(0, groups, earlier, jnp.zeros((cap, LANES), jnp.float32))
        blocks = lax.broadcasted_iota(jnp.int32, (cap, nb), 1)
        one = jnp.where(mine[:, :nb] == blocks, 1.0, 0.0)
        first = one * (1.0 - dup[:, :nb])
        both = jnp.concatenate([one, first], axis=0).T
        one, first = both[:, :cap], both[:, cap:]
        hot[...] = jnp.concatenate([one, one], axis=1).astype(jnp.bfloat16)
        rep[...] = jnp.concatenate([first] * 4, axis=1).astype(jnp.bfloat16)

    init_pot[...] = tinit[...] * SCALE
    prepare(rows, seg_s, hot_s, rep_s)
    prepare(cols, seg_t, hot_t, rep_t)

    def row_pass(pot, first):
        def group(g, acc):
            base = g * GROUP
            if first:
                fetch(g).wait()
            for k in range(GROUP):
                s = base + k
                tile = cbuf[s]
                if first:
                    tile = tile * SCALE
                    cbuf[s] = tile
                x = pot[pl.ds(cols[0, 0, s], 1), :] - tile
                m = jnp.max(x, axis=1, keepdims=True)
                t = jnp.sum(jnp.exp2(x - m), axis=1, keepdims=True)
                acc = jnp.where(lane == s, m + jnp.log2(t), acc)
            return acc

        acc = lax.fori_loop(0, groups, group, jnp.zeros((LANES, LANES), jnp.float32))
        lbuf[...] = acc.T[:cap]

    def col_pass(pot):
        def collect(g, _):
            for k in range(GROUP):
                s = g * GROUP + k
                gbuf[pl.ds(s, 1), :] = pot[pl.ds(rows[0, 0, s], 1), :]
            return 0

        lax.fori_loop(0, groups, collect, 0)
        turned = gbuf[...].T

        def group(g, _):
            base = g * GROUP
            near = pltpu.roll(turned, lax.rem(LANES - base, LANES), 1)
            top = jnp.zeros((GROUP, LANES), jnp.float32)
            mass = jnp.ones((GROUP, LANES), jnp.float32)
            for k in range(GROUP):
                x = near[:, k : k + 1] - cbuf[base + k]
                m = jnp.max(x, axis=0, keepdims=True)
                t = jnp.sum(jnp.exp2(x - m), axis=0, keepdims=True)
                top = jnp.where(sub8 == k, m, top)
                mass = jnp.where(sub8 == k, t, mass)
            lbuf[pl.ds(pl.multiple_of(base, GROUP), GROUP), :] = top + jnp.log2(mass)
            return 0

        lax.fori_loop(0, groups, group, 0)

    def merge(ids, seg, hot, rep, part):
        mine = seg[...]
        own = lbuf[...]

        def widen(g, best):
            for k in range(GROUP):
                t = g * GROUP + k
                other = jnp.maximum(best, lbuf[pl.ds(t, 1), :])
                best = jnp.where(mine == segment(ids, t), other, best)
            return best

        best = lax.fori_loop(0, groups, widen, own)
        weight = jnp.concatenate(split_bf16(jnp.exp2(own - best), 2), axis=0)
        tops = split_bf16(best, 3)
        tops = jnp.concatenate(tops + [jnp.zeros_like(tops[0])], axis=0)
        mass = jnp.dot(hot[...], weight, preferred_element_type=jnp.float32)
        peak = jnp.dot(rep[...], tops, preferred_element_type=jnp.float32)
        part[...] = jnp.where(mass > 0.0, peak + jnp.log2(mass), -1e30)

    pending = []

    def exchange(axis, it, part, mid, pot, logmass, s_send, s_recv, g_send, g_recv):
        n = sizes[axis]
        chunk = part.shape[0] // n
        copies = []
        for o in range(1, n):
            to = peer(axis, o)
            copies.append(pltpu.make_async_remote_copy(
                src_ref=part.at[pl.ds(to * chunk, chunk)],
                dst_ref=mid.at[o - 1],
                send_sem=s_send.at[it, o - 1],
                recv_sem=s_recv.at[it, o - 1],
                device_id={axis: to},
                device_id_type=MESH,
            ))
            copies[-1].start()
        own = pl.ds(pl.multiple_of(me[axis] * chunk, chunk), chunk)
        parts = [part[own, :]]
        mass = logmass[own, :] * LOG2E
        for copy in copies:
            copy.wait_recv()
        parts += [mid[o] for o in range(n - 1)]
        top = functools.reduce(jnp.maximum, parts)
        total = functools.reduce(jnp.add, [jnp.exp2(p - top) for p in parts])
        pot[own, :] = mass - (top + jnp.log2(total))
        pending.extend(copies)
        copies = []
        for o in range(1, n):
            copies.append(pltpu.make_async_remote_copy(
                src_ref=pot.at[own],
                dst_ref=pot.at[own],
                send_sem=g_send.at[it, o - 1],
                recv_sem=g_recv.at[it, o - 1],
                device_id={axis: peer(axis, o)},
                device_id_type=MESH,
            ))
            copies[-1].start()
        for copy in copies:
            copy.wait_recv()
        pending.extend(copies)

    source = ((part_s0, mid_s0, pot_s0), (part_s1, mid_s1, pot_s1))
    target = ((part_t0, mid_t0, pot_t0), (part_t1, mid_t1, pot_t1))
    pot = init_pot
    for it in range(ITERS):
        part, mid, pot_s = source[it]
        row_pass(pot, it == 0)
        merge(rows, seg_s, hot_s, rep_s, part)
        if it == 0:
            pl.semaphore_wait(barrier, n_row + n_col - 2)
        exchange("col", it, part, mid, pot_s, slog,
                 scatter_send_s, scatter_recv_s, gather_send_s, gather_recv_s)
        part, mid, pot = target[it]
        col_pass(pot_s)
        merge(cols, seg_t, hot_t, rep_t, part)
        exchange("row", it, part, mid, pot, tlog,
                 scatter_send_t, scatter_recv_t, gather_send_t, gather_recv_t)
    s_out[...] = pot_s[...]
    t_out[...] = pot[...]
    for copy in pending:
        copy.wait_send()


def local(
    n_row, n_col,
    cost_tiles, tile_rows, tile_cols, tile_count, source_logmass, target_logmass, target_init,
):
    cap, width = cost_tiles.shape[2], cost_tiles.shape[-1]
    nbs = source_logmass.shape[0] // width
    nbt = target_logmass.shape[0] // width
    f32, bf16 = jnp.float32, jnp.bfloat16
    vmem = pl.BlockSpec(memory_space=pltpu.VMEM)
    smem = pl.BlockSpec(memory_space=pltpu.SMEM)
    dma = pltpu.SemaphoreType.DMA
    scratch = [
        pltpu.VMEM((cap, width, width), f32),
        pltpu.VMEM((cap, width), f32),
        pltpu.VMEM((cap, width), f32),
        pltpu.VMEM((nbt, width), f32),
        pltpu.VMEM((cap, width), jnp.int32),
        pltpu.VMEM((cap, width), jnp.int32),
        pltpu.VMEM((nbs, 2 * cap), bf16),
        pltpu.VMEM((nbt, 2 * cap), bf16),
        pltpu.VMEM((nbs, 4 * cap), bf16),
        pltpu.VMEM((nbt, 4 * cap), bf16),
    ]
    scratch += [pltpu.VMEM((nbs, width), f32)] * 2 + [pltpu.VMEM((nbt, width), f32)] * 2
    scratch += [pltpu.VMEM((n_col - 1, nbs // n_col, width), f32)] * 2
    scratch += [pltpu.VMEM((n_row - 1, nbt // n_row, width), f32)] * 2
    scratch += [pltpu.VMEM((nbs, width), f32)] * 2 + [pltpu.VMEM((nbt, width), f32)] * 2
    scratch += [dma((cap // GROUP,))]
    scratch += [dma((ITERS, n_col - 1))] * 4 + [dma((ITERS, n_row - 1))] * 4
    source, target = pl.pallas_call(
        functools.partial(kernel, n_row=n_row, n_col=n_col),
        out_shape=(
            jax.ShapeDtypeStruct((nbs, width), f32),
            jax.ShapeDtypeStruct((nbt, width), f32),
        ),
        in_specs=[pl.BlockSpec(memory_space=pl.ANY), smem, smem, smem, vmem, vmem, vmem],
        out_specs=(vmem, vmem),
        scratch_shapes=scratch,
        compiler_params=pltpu.CompilerParams(
            collective_id=0, has_side_effects=True, vmem_limit_bytes=48 * 1024 * 1024
        ),
        cost_estimate=pl.CostEstimate(
            flops=2 * ITERS * 5 * cap * width * width,
            bytes_accessed=4 * cap * width * width,
            transcendentals=2 * ITERS * cap * width * width,
        ),
    )(
        cost_tiles, tile_rows, tile_cols, tile_count,
        source_logmass.reshape(nbs, width),
        target_logmass.reshape(nbt, width),
        target_init.reshape(nbt, width),
    )
    return source.reshape(-1) / SCALE, target.reshape(-1) / SCALE


def solution(mesh):
    return jax.shard_map(
        functools.partial(local, mesh.shape["row"], mesh.shape["col"]),
        mesh=mesh,
        in_specs=(
            P("row", "col", None, None, None),
            P("row", "col", None),
            P("row", "col", None),
            P("row", "col"),
            P("row"),
            P("col"),
            P("col"),
        ),
        out_specs=(P("row"), P("col")),
        check_vma=False,
    )
```

```python
import functools
import math

import jax
import jax.numpy as jnp
from jax import lax
from jax.experimental import pallas as pl
from jax.experimental.pallas import tpu as pltpu
from jax.sharding import PartitionSpec as P

ITERS = 2
EPS = 0.1
LOG2E = math.log2(math.e)
SCALE = LOG2E / EPS
GROUP = 8
LANES = 128
MESH = pl.DeviceIdType.MESH


def join(parts):
    top = functools.reduce(jnp.maximum, parts)
    total = functools.reduce(jnp.add, [jnp.exp2(p - top) for p in parts])
    return top + jnp.log2(total)


def split_bf16(x, parts):
    out = []
    for _ in range(parts):
        head = x.astype(jnp.bfloat16)
        out.append(head)
        x = x - head.astype(jnp.float32)
    return out


def kernel(
    cost, rows_in, cols_in, count, slog_in, tlog_in, tinit_in,
    s_out, t_out,
    rows, cols, slog, tlog, small_sem,
    cbuf, turned_cost, fine, lbuf, gbuf, init_pot, seg_s, seg_t, hot_s, hot_t, rep_s, rep_t,
    part_s0, part_s1, part_t0, part_t1,
    mid_s0, mid_s1, mid_t0, mid_t1,
    pot_s0, pot_s1, pot_t0, pot_t1,
    cost_sem, scatter_send_s, scatter_recv_s, gather_send_s, gather_recv_s,
    scatter_send_t, scatter_recv_t, gather_send_t, gather_recv_t,
    *, n_row, n_col,
):
    cap = cbuf.shape[0]
    me = {"row": lax.axis_index("row"), "col": lax.axis_index("col")}
    sizes = {"row": n_row, "col": n_col}

    def peer(axis, o):
        return lax.rem(me[axis] + o, sizes[axis])

    barrier = pltpu.get_barrier_semaphore()
    for axis in ("col", "row"):
        for o in range(1, sizes[axis]):
            pl.semaphore_signal(
                barrier, inc=1, device_id={axis: peer(axis, o)}, device_id_type=MESH
            )

    groups = cap // GROUP

    def fetch(g):
        span = pl.ds(g * GROUP, GROUP)
        return pltpu.make_async_copy(cost.at[0, 0, span], cbuf.at[span], cost_sem.at[g])

    small = [
        pltpu.make_async_copy(src, dst, small_sem.at[k])
        for k, (src, dst) in enumerate((
            (rows_in, rows), (cols_in, cols), (tinit_in, init_pot), (slog_in, slog), (tlog_in, tlog),
        ))
    ]
    for copy in small:
        copy.start()
    for g in range(groups):
        fetch(g).start()

    total = count[0, 0]
    lane = lax.broadcasted_iota(jnp.int32, (LANES, LANES), 1)
    sub8 = lax.broadcasted_iota(jnp.int32, (GROUP, LANES), 0)
    slot = lax.broadcasted_iota(jnp.int32, (cap, LANES), 0)

    def segment(ids, s):
        return jnp.where(s < total, ids[0, 0, s], -1)

    def prepare(ids, seg, hot, rep):
        nb = hot.shape[0]

        def fill(g, _):
            value = jnp.zeros((GROUP, LANES), jnp.int32)
            for k in range(GROUP):
                value = jnp.where(sub8 == k, segment(ids, g * GROUP + k), value)
            seg[pl.ds(pl.multiple_of(g * GROUP, GROUP), GROUP), :] = value
            return 0

        lax.fori_loop(0, groups, fill, 0)
        mine = seg[...]

        def earlier(g, dup):
            for k in range(GROUP):
                t = g * GROUP + k
                same = (mine == segment(ids, t)) & (slot > t)
                dup = jnp.where(same, 1.0, dup)
            return dup

        dup = lax.fori_loop(0, groups, earlier, jnp.zeros((cap, LANES), jnp.float32))
        blocks = lax.broadcasted_iota(jnp.int32, (cap, nb), 1)
        one = jnp.where(mine[:, :nb] == blocks, 1.0, 0.0)
        first = one * (1.0 - dup[:, :nb])
        both = jnp.concatenate([one, first], axis=0).T
        one, first = both[:, :cap], both[:, cap:]
        hot[...] = jnp.concatenate([one, one], axis=1).astype(jnp.bfloat16)
        rep[...] = jnp.concatenate([first] * 4, axis=1).astype(jnp.bfloat16)

    gbuf[...] = jnp.zeros_like(gbuf)
    for copy in small:
        copy.wait()
    init_pot[...] = init_pot[...] * SCALE
    prepare(rows, seg_s, hot_s, rep_s)
    prepare(cols, seg_t, hot_t, rep_t)

    def lse_pass(pot, ids, tiles, first):
        def collect(g, _):
            for k in range(GROUP):
                s = g * GROUP + k
                gbuf[pl.ds(s, 1), :] = pot[pl.ds(ids[0, 0, s], 1), :]
            return 0

        lax.fori_loop(0, groups, collect, 0)
        turned = gbuf[...].T

        def group(g, _):
            base = g * GROUP
            near = pltpu.roll(turned, lax.rem(LANES - base, LANES), 1)
            if first:
                fetch(g).wait()
                for k in range(GROUP):
                    tile = cbuf[base + k] * SCALE
                    cbuf[base + k] = tile
                    tiles[base + k] = tile.T
            for k in range(GROUP):
                x = near[:, k : k + 1] - tiles[base + k]
                x = x.reshape(LANES // GROUP, GROUP, LANES)
                m = jnp.max(x, axis=0)
                t = jnp.sum(jnp.exp2(x - m[None]), axis=0)
                row = pl.multiple_of((base + k) * GROUP, GROUP)
                fine[pl.ds(row, GROUP), :] = m + jnp.log2(t)
            return 0

        lax.fori_loop(0, groups, group, 0)
        pieces = [fine[pl.ds(k, cap, stride=GROUP), :] for k in range(GROUP)]
        lbuf[...] = join(pieces)

    def merge(ids, seg, hot, rep, part):
        mine = seg[...]
        own = lbuf[...]

        def widen(g, best):
            for k in range(GROUP):
                t = g * GROUP + k
                other = jnp.maximum(best, lbuf[pl.ds(t, 1), :])
                best = jnp.where(mine == segment(ids, t), other, best)
            return best

        best = lax.fori_loop(0, groups, widen, own)
        weight = jnp.concatenate(split_bf16(jnp.exp2(own - best), 2), axis=0)
        tops = split_bf16(best, 3)
        tops = jnp.concatenate(tops + [jnp.zeros_like(tops[0])], axis=0)
        mass = jnp.dot(hot[...], weight, preferred_element_type=jnp.float32)
        peak = jnp.dot(rep[...], tops, preferred_element_type=jnp.float32)
        part[...] = jnp.where(mass > 0.0, peak + jnp.log2(mass), -1e30)

    pending = []

    def exchange(axis, it, part, mid, pot, logmass, s_send, s_recv, g_send, g_recv):
        n = sizes[axis]
        chunk = part.shape[0] // n
        copies = []
        for o in range(1, n):
            to = peer(axis, o)
            copies.append(pltpu.make_async_remote_copy(
                src_ref=part.at[pl.ds(to * chunk, chunk)],
                dst_ref=mid.at[o - 1],
                send_sem=s_send.at[it, o - 1],
                recv_sem=s_recv.at[it, o - 1],
                device_id={axis: to},
                device_id_type=MESH,
            ))
            copies[-1].start()
        own = pl.ds(pl.multiple_of(me[axis] * chunk, chunk), chunk)
        parts = [part[own, :]]
        mass = logmass[own, :] * LOG2E
        for copy in copies:
            copy.wait_recv()
        parts += [mid[o] for o in range(n - 1)]
        pot[own, :] = mass - join(parts)
        pending.extend(copies)
        copies = []
        for o in range(1, n):
            copies.append(pltpu.make_async_remote_copy(
                src_ref=pot.at[own],
                dst_ref=pot.at[own],
                send_sem=g_send.at[it, o - 1],
                recv_sem=g_recv.at[it, o - 1],
                device_id={axis: peer(axis, o)},
                device_id_type=MESH,
            ))
            copies[-1].start()
        for copy in copies:
            copy.wait_recv()
        pending.extend(copies)

    source = ((part_s0, mid_s0, pot_s0), (part_s1, mid_s1, pot_s1))
    target = ((part_t0, mid_t0, pot_t0), (part_t1, mid_t1, pot_t1))
    pot = init_pot
    for it in range(ITERS):
        part, mid, pot_s = source[it]
        lse_pass(pot, cols, turned_cost, it == 0)
        merge(rows, seg_s, hot_s, rep_s, part)
        if it == 0:
            pl.semaphore_wait(barrier, n_row + n_col - 2)
        exchange("col", it, part, mid, pot_s, slog,
                 scatter_send_s, scatter_recv_s, gather_send_s, gather_recv_s)
        part, mid, pot = target[it]
        lse_pass(pot_s, rows, cbuf, False)
        merge(cols, seg_t, hot_t, rep_t, part)
        exchange("row", it, part, mid, pot, tlog,
                 scatter_send_t, scatter_recv_t, gather_send_t, gather_recv_t)
    s_out[...] = pot_s[...]
    t_out[...] = pot[...]
    for copy in pending:
        copy.wait_send()


def local(
    n_row, n_col,
    cost_tiles, tile_rows, tile_cols, tile_count, source_logmass, target_logmass, target_init,
):
    cap, width = cost_tiles.shape[2], cost_tiles.shape[-1]
    nbs = source_logmass.shape[0] // width
    nbt = target_logmass.shape[0] // width
    f32, bf16 = jnp.float32, jnp.bfloat16
    hbm = pl.BlockSpec(memory_space=pltpu.HBM)
    vmem = pl.BlockSpec(memory_space=pltpu.VMEM)
    smem = pl.BlockSpec(memory_space=pltpu.SMEM)
    dma = pltpu.SemaphoreType.DMA
    scratch = [
        pltpu.SMEM((1, 1, cap), jnp.int32),
        pltpu.SMEM((1, 1, cap), jnp.int32),
        pltpu.VMEM((nbs, width), f32),
        pltpu.VMEM((nbt, width), f32),
        dma((5,)),
        pltpu.VMEM((cap, width, width), f32),
        pltpu.VMEM((cap, width, width), f32),
        pltpu.VMEM((cap * GROUP, width), f32),
        pltpu.VMEM((cap, width), f32),
        pltpu.VMEM((width, width), f32),
        pltpu.VMEM((nbt, width), f32),
        pltpu.VMEM((cap, width), jnp.int32),
        pltpu.VMEM((cap, width), jnp.int32),
        pltpu.VMEM((nbs, 2 * cap), bf16),
        pltpu.VMEM((nbt, 2 * cap), bf16),
        pltpu.VMEM((nbs, 4 * cap), bf16),
        pltpu.VMEM((nbt, 4 * cap), bf16),
    ]
    scratch += [pltpu.VMEM((nbs, width), f32)] * 2 + [pltpu.VMEM((nbt, width), f32)] * 2
    scratch += [pltpu.VMEM((n_col - 1, nbs // n_col, width), f32)] * 2
    scratch += [pltpu.VMEM((n_row - 1, nbt // n_row, width), f32)] * 2
    scratch += [pltpu.VMEM((nbs, width), f32)] * 2 + [pltpu.VMEM((nbt, width), f32)] * 2
    scratch += [dma((cap // GROUP,))]
    scratch += [dma((ITERS, n_col - 1))] * 4 + [dma((ITERS, n_row - 1))] * 4
    source, target = pl.pallas_call(
        functools.partial(kernel, n_row=n_row, n_col=n_col),
        out_shape=(
            jax.ShapeDtypeStruct((nbs, width), f32),
            jax.ShapeDtypeStruct((nbt, width), f32),
        ),
        in_specs=[hbm, hbm, hbm, smem, hbm, hbm, hbm],
        out_specs=(vmem, vmem),
        scratch_shapes=scratch,
        compiler_params=pltpu.CompilerParams(
            collective_id=0, has_side_effects=True, vmem_limit_bytes=65536 * 1024
        ),
        cost_estimate=pl.CostEstimate(
            flops=2 * ITERS * 5 * cap * width * width,
            bytes_accessed=4 * cap * width * width,
            transcendentals=2 * ITERS * cap * width * width,
        ),
    )(
        cost_tiles, tile_rows, tile_cols, tile_count,
        source_logmass.reshape(nbs, width),
        target_logmass.reshape(nbt, width),
        target_init.reshape(nbt, width),
    )
    return source.reshape(-1) / SCALE, target.reshape(-1) / SCALE


def solution(mesh):
    return jax.shard_map(
        functools.partial(local, mesh.shape["row"], mesh.shape["col"]),
        mesh=mesh,
        in_specs=(
            P("row", "col", None, None, None),
            P("row", "col", None),
            P("row", "col", None),
            P("row", "col"),
            P("row"),
            P("col"),
            P("col"),
        ),
        out_specs=(P("row"), P("col")),
        check_vma=False,
    )
```

```python
import functools
import math

import jax
import jax.numpy as jnp
from jax import lax
from jax.experimental import pallas as pl
from jax.experimental.pallas import tpu as pltpu
from jax.sharding import PartitionSpec as P

ITERS = 2
EPS = 0.1
LOG2E = math.log2(math.e)
SCALE = LOG2E / EPS
GROUP = 8
TILES = 16
LANES = 128
MESH = pl.DeviceIdType.MESH


def join(parts):
    top = functools.reduce(jnp.maximum, parts)
    total = functools.reduce(jnp.add, [jnp.exp2(p - top) for p in parts])
    return top + jnp.log2(total)


def split_bf16(x, parts):
    out = []
    for _ in range(parts):
        head = x.astype(jnp.bfloat16)
        out.append(head)
        x = x - head.astype(jnp.float32)
    return out


def kernel(
    cost, rows_in, cols_in, count, slog_in, tlog_in, tinit_in,
    s_out, t_out,
    rows, cols, slog, tlog, small_sem,
    cbuf, turned_cost, fine, lbuf, gbuf, init_pot, seg_s, seg_t,
    same_s, first_s, first_in, place_s, absent_s, hot_t, rep_t,
    slots_s0, slots_s1, part_t0, part_t1,
    mid_s0, mid_s1, mid_t0, mid_t1,
    pot_s0, pot_s1, pot_t0, pot_t1,
    cost_sem, first_send, first_recv, slots_send, slots_recv,
    scatter_send_t, scatter_recv_t, gather_send_t, gather_recv_t, out_sem,
    *, n_row, n_col,
):
    cap = cbuf.shape[0]
    me = {"row": lax.axis_index("row"), "col": lax.axis_index("col")}
    sizes = {"row": n_row, "col": n_col}

    def peer(axis, o):
        return lax.rem(me[axis] + o, sizes[axis])

    barrier = pltpu.get_barrier_semaphore()
    for axis in ("col", "row"):
        for o in range(1, sizes[axis]):
            pl.semaphore_signal(
                barrier, inc=1, device_id={axis: peer(axis, o)}, device_id_type=MESH
            )

    groups = cap // TILES

    def fetch(g):
        span = pl.ds(g * TILES, TILES)
        return pltpu.make_async_copy(cost.at[0, 0, span], cbuf.at[span], cost_sem.at[g])

    small = [
        pltpu.make_async_copy(src, dst, small_sem.at[k])
        for k, (src, dst) in enumerate((
            (rows_in, rows), (cols_in, cols), (tinit_in, init_pot), (slog_in, slog), (tlog_in, tlog),
        ))
    ]
    for copy in small:
        copy.start()
    for g in range(groups):
        fetch(g).start()

    total = count[0, 0]
    lane = lax.broadcasted_iota(jnp.int32, (LANES, LANES), 1)
    sub8 = lax.broadcasted_iota(jnp.int32, (GROUP, LANES), 0)
    slot = lax.broadcasted_iota(jnp.int32, (cap, LANES), 0)

    def segment(ids, s):
        return jnp.where(s < total, ids[0, 0, s], -1)

    def prepare(ids, seg, nb):
        def fill(g, _):
            value = jnp.zeros((GROUP, LANES), jnp.int32)
            for k in range(GROUP):
                value = jnp.where(sub8 == k, segment(ids, g * GROUP + k), value)
            seg[pl.ds(pl.multiple_of(g * GROUP, GROUP), GROUP), :] = value
            return 0

        lax.fori_loop(0, cap // GROUP, fill, 0)
        mine = seg[...]

        def earlier(g, dup):
            for k in range(GROUP):
                t = g * GROUP + k
                same = (mine == segment(ids, t)) & (slot > t)
                dup = jnp.where(same, 1.0, dup)
            return dup

        dup = jnp.zeros((cap, LANES), jnp.float32)
        dup = lax.fori_loop(0, cap // GROUP, earlier, dup)
        blocks = lax.broadcasted_iota(jnp.int32, (cap, nb), 1)
        one = jnp.where(mine[:, :nb] == blocks, 1.0, 0.0)
        return one, one * (1.0 - dup[:, :nb])

    def prepare_source():
        one, first = prepare(rows, seg_s, first_s.shape[1])
        first_s[...] = first
        one = one.astype(jnp.bfloat16)
        same = lax.dot_general(
            one, one, (((1,), (1,)), ((), ())), preferred_element_type=jnp.float32
        )
        same_s[...] = jnp.concatenate([same, same], axis=1).astype(jnp.bfloat16)

    def prepare_target():
        one, first = prepare(cols, seg_t, hot_t.shape[0])
        both = jnp.concatenate([one, first], axis=0).T
        one, first = both[:, :cap], both[:, cap:]
        hot_t[...] = jnp.concatenate([one, one], axis=1).astype(jnp.bfloat16)
        rep_t[...] = jnp.concatenate([first] * 4, axis=1).astype(jnp.bfloat16)

    def prepare_place(q, first):
        first = first.T
        place_s[q] = jnp.concatenate([first] * 4, axis=1).astype(jnp.bfloat16)
        found = jnp.sum(first, axis=1, keepdims=True)
        absent_s[q] = jnp.broadcast_to(jnp.where(found > 0.0, 0.0, -1e30), absent_s.shape[1:])

    gbuf[...] = jnp.zeros_like(gbuf)
    for copy in small:
        copy.wait()
    init_pot[...] = init_pot[...] * SCALE
    prepare_source()

    def lse_pass(pot, ids, tiles, first):
        def collect(g, _):
            for k in range(TILES):
                s = g * TILES + k
                gbuf[pl.ds(s, 1), :] = pot[pl.ds(ids[0, 0, s], 1), :]
            return 0

        lax.fori_loop(0, groups, collect, 0)
        turned = gbuf[...].T

        def group(g, _):
            base = g * TILES
            near = pltpu.roll(turned, lax.rem(LANES - base, LANES), 1)
            if first:
                fetch(g).wait()
                for k in range(TILES):
                    tile = cbuf[base + k] * SCALE
                    cbuf[base + k] = tile
                    tiles[base + k] = tile.T
            for k in range(TILES):
                x = near[:, k : k + 1] - tiles[base + k]
                x = x.reshape(LANES // GROUP, GROUP, LANES)
                m = jnp.max(x, axis=0)
                t = jnp.sum(jnp.exp2(x - m[None]), axis=0)
                row = pl.multiple_of((base + k) * GROUP, GROUP)
                fine[pl.ds(row, GROUP), :] = m + jnp.log2(t)
            return 0

        lax.fori_loop(0, groups, group, 0)
        pieces = [fine[pl.ds(k, cap, stride=GROUP), :] for k in range(GROUP)]
        lbuf[...] = join(pieces)

    def level(ids, seg):
        mine = seg[...]
        own = lbuf[...]

        def widen(g, best):
            for k in range(GROUP):
                t = g * GROUP + k
                other = jnp.maximum(best, lbuf[pl.ds(t, 1), :])
                best = jnp.where(mine == segment(ids, t), other, best)
            return best

        best = lax.fori_loop(0, cap // GROUP, widen, own)
        return best, jnp.concatenate(split_bf16(jnp.exp2(own - best), 2), axis=0)

    def thirds(x):
        parts = split_bf16(x, 3)
        return jnp.concatenate(parts + [jnp.zeros_like(parts[0])], axis=0)

    def merge_source(slots):
        best, weight = level(rows, seg_s)
        mass = jnp.dot(same_s[...], weight, preferred_element_type=jnp.float32)
        slots[...] = best + jnp.log2(jnp.maximum(mass, 1.0))

    def merge_target(part):
        best, weight = level(cols, seg_t)
        mass = jnp.dot(hot_t[...], weight, preferred_element_type=jnp.float32)
        peak = jnp.dot(rep_t[...], thirds(best), preferred_element_type=jnp.float32)
        part[...] = jnp.where(mass > 0.0, peak + jnp.log2(mass), -1e30)

    pending = []

    def send_all(axis, src, inbox, send, recv):
        copies = []
        for o in range(1, sizes[axis]):
            copies.append(pltpu.make_async_remote_copy(
                src_ref=src,
                dst_ref=inbox.at[o - 1],
                send_sem=send.at[o - 1],
                recv_sem=recv.at[o - 1],
                device_id={axis: peer(axis, o)},
                device_id_type=MESH,
            ))
            copies[-1].start()
        pending.extend(copies)
        return copies

    def place(q, slots):
        spread = jnp.dot(place_s[q], thirds(slots), preferred_element_type=jnp.float32)
        return spread + absent_s[q]

    def exchange(axis, it, part, mid, pot, logmass, s_send, s_recv, g_send, g_recv):
        n = sizes[axis]
        chunk = part.shape[0] // n
        copies = []
        for o in range(1, n):
            to = peer(axis, o)
            copies.append(pltpu.make_async_remote_copy(
                src_ref=part.at[pl.ds(to * chunk, chunk)],
                dst_ref=mid.at[o - 1],
                send_sem=s_send.at[it, o - 1],
                recv_sem=s_recv.at[it, o - 1],
                device_id={axis: to},
                device_id_type=MESH,
            ))
            copies[-1].start()
        own = pl.ds(pl.multiple_of(me[axis] * chunk, chunk), chunk)
        parts = [part[own, :]]
        mass = logmass[own, :] * LOG2E
        for copy in copies:
            copy.wait_recv()
        parts += [mid[o] for o in range(n - 1)]
        pot[own, :] = mass - join(parts)
        pending.extend(copies)
        copies = []
        for o in range(1, n):
            copies.append(pltpu.make_async_remote_copy(
                src_ref=pot.at[own],
                dst_ref=pot.at[own],
                send_sem=g_send.at[it, o - 1],
                recv_sem=g_recv.at[it, o - 1],
                device_id={axis: peer(axis, o)},
                device_id_type=MESH,
            ))
            copies[-1].start()
        for copy in copies:
            copy.wait_recv()
        pending.extend(copies)

    pl.semaphore_wait(barrier, n_row + n_col - 2)
    firsts = send_all("col", first_s, first_in, first_send, first_recv)
    prepare_place(0, first_s[...])

    source = ((slots_s0, mid_s0, pot_s0), (slots_s1, mid_s1, pot_s1))
    target = ((part_t0, mid_t0, pot_t0), (part_t1, mid_t1, pot_t1))
    pot = init_pot
    for it in range(ITERS):
        slots, inbox, pot_s = source[it]
        lse_pass(pot, cols, turned_cost, it == 0)
        merge_source(slots)
        copies = send_all("col", slots, inbox, slots_send.at[it], slots_recv.at[it])
        if it == 0:
            prepare_target()
            for q, copy in enumerate(firsts):
                copy.wait_recv()
                prepare_place(q + 1, first_in[q])
        parts = [place(0, slots[...])]
        for q, copy in enumerate(copies):
            copy.wait_recv()
            parts.append(place(q + 1, inbox[q]))
        pot_s[...] = slog[...] * LOG2E - join(parts)
        if it == ITERS - 1:
            out_copy = pltpu.make_async_copy(pot_s, s_out, out_sem.at[0])
            out_copy.start()
        part, mid, pot = target[it]
        lse_pass(pot_s, rows, cbuf, False)
        merge_target(part)
        exchange("row", it, part, mid, pot, tlog,
                 scatter_send_t, scatter_recv_t, gather_send_t, gather_recv_t)
    last_copy = pltpu.make_async_copy(pot, t_out, out_sem.at[1])
    last_copy.start()
    for copy in pending:
        copy.wait_send()
    out_copy.wait()
    last_copy.wait()


def local(
    n_row, n_col,
    cost_tiles, tile_rows, tile_cols, tile_count, source_logmass, target_logmass, target_init,
):
    cap, width = cost_tiles.shape[2], cost_tiles.shape[-1]
    nbs = source_logmass.shape[0] // width
    nbt = target_logmass.shape[0] // width
    f32, bf16 = jnp.float32, jnp.bfloat16
    hbm = pl.BlockSpec(memory_space=pltpu.HBM)
    smem = pl.BlockSpec(memory_space=pltpu.SMEM)
    dma = pltpu.SemaphoreType.DMA
    scratch = [
        pltpu.SMEM((1, 1, cap), jnp.int32),
        pltpu.SMEM((1, 1, cap), jnp.int32),
        pltpu.VMEM((nbs, width), f32),
        pltpu.VMEM((nbt, width), f32),
        dma((5,)),
        pltpu.VMEM((cap, width, width), f32),
        pltpu.VMEM((cap, width, width), f32),
        pltpu.VMEM((cap * GROUP, width), f32),
        pltpu.VMEM((cap, width), f32),
        pltpu.VMEM((width, width), f32),
        pltpu.VMEM((nbt, width), f32),
        pltpu.VMEM((cap, width), jnp.int32),
        pltpu.VMEM((cap, width), jnp.int32),
        pltpu.VMEM((cap, 2 * cap), bf16),
        pltpu.VMEM((cap, nbs), f32),
        pltpu.VMEM((n_col - 1, cap, nbs), f32),
        pltpu.VMEM((n_col, nbs, 4 * cap), bf16),
        pltpu.VMEM((n_col, nbs, width), f32),
        pltpu.VMEM((nbt, 2 * cap), bf16),
        pltpu.VMEM((nbt, 4 * cap), bf16),
    ]
    scratch += [pltpu.VMEM((cap, width), f32)] * 2 + [pltpu.VMEM((nbt, width), f32)] * 2
    scratch += [pltpu.VMEM((n_col - 1, cap, width), f32)] * 2
    scratch += [pltpu.VMEM((n_row - 1, nbt // n_row, width), f32)] * 2
    scratch += [pltpu.VMEM((nbs, width), f32)] * 2 + [pltpu.VMEM((nbt, width), f32)] * 2
    scratch += [dma((cap // TILES,))]
    scratch += [dma((n_col - 1,))] * 2 + [dma((ITERS, n_col - 1))] * 2
    scratch += [dma((ITERS, n_row - 1))] * 4 + [dma((2,))]
    source, target = pl.pallas_call(
        functools.partial(kernel, n_row=n_row, n_col=n_col),
        out_shape=(
            jax.ShapeDtypeStruct((nbs, width), f32),
            jax.ShapeDtypeStruct((nbt, width), f32),
        ),
        in_specs=[hbm, hbm, hbm, smem, hbm, hbm, hbm],
        out_specs=(hbm, hbm),
        scratch_shapes=scratch,
        compiler_params=pltpu.CompilerParams(
            collective_id=0, has_side_effects=True, vmem_limit_bytes=65536 * 1024
        ),
        cost_estimate=pl.CostEstimate(
            flops=2 * ITERS * 5 * cap * width * width,
            bytes_accessed=4 * cap * width * width,
            transcendentals=2 * ITERS * cap * width * width,
        ),
    )(
        cost_tiles, tile_rows, tile_cols, tile_count,
        source_logmass.reshape(nbs, width),
        target_logmass.reshape(nbt, width),
        target_init.reshape(nbt, width),
    )
    return source.reshape(-1) / SCALE, target.reshape(-1) / SCALE


def solution(mesh):
    return jax.shard_map(
        functools.partial(local, mesh.shape["row"], mesh.shape["col"]),
        mesh=mesh,
        in_specs=(
            P("row", "col", None, None, None),
            P("row", "col", None),
            P("row", "col", None),
            P("row", "col"),
            P("row"),
            P("col"),
            P("col"),
        ),
        out_specs=(P("row"), P("col")),
        check_vma=False,
    )
```

```python
import functools
import math

import jax
import jax.numpy as jnp
from jax import lax
from jax.experimental import pallas as pl
from jax.experimental.pallas import tpu as pltpu
from jax.sharding import PartitionSpec as P

ITERS = 2
EPS = 0.1
LOG2E = math.log2(math.e)
SCALE = LOG2E / EPS
GROUP = 8
TILES = 16
WIDE = 32
LANES = 128
MESH = pl.DeviceIdType.MESH


def join(parts):
    top = functools.reduce(jnp.maximum, parts)
    total = functools.reduce(jnp.add, [jnp.exp2(p - top) for p in parts])
    return top + jnp.log2(total)


def split_bf16(x, parts):
    out = []
    for _ in range(parts):
        head = x.astype(jnp.bfloat16)
        out.append(head)
        x = x - head.astype(jnp.float32)
    return out


def kernel(
    cost, rows_in, cols_in, count, slog_in, tlog_in, tinit_in,
    s_out, t_out,
    rows, cols, slog, tlog, small_sem,
    cbuf, turned_cost, fine, lbuf, gbuf, near, moved, init_pot, seg_s, seg_t,
    same_s, first_s, first_in, place_s, absent_s, hot_t, rep_t,
    slots_s0, slots_s1, part_t0, part_t1,
    mid_s0, mid_s1, mid_t0, mid_t1,
    pot_s0, pot_s1, pot_t0, pot_t1,
    cost_sem, first_send, first_recv, slots_send, slots_recv,
    scatter_send_t, scatter_recv_t, gather_send_t, gather_recv_t,
    *, n_row, n_col,
):
    cap = cbuf.shape[0]
    me = {"row": lax.axis_index("row"), "col": lax.axis_index("col")}
    sizes = {"row": n_row, "col": n_col}

    def peer(axis, o):
        return lax.rem(me[axis] + o, sizes[axis])

    barrier = pltpu.get_barrier_semaphore()
    for axis in ("col", "row"):
        for o in range(1, sizes[axis]):
            pl.semaphore_signal(
                barrier, inc=1, device_id={axis: peer(axis, o)}, device_id_type=MESH
            )

    groups = cap // TILES

    def fetch(g):
        span = pl.ds(g * TILES, TILES)
        return pltpu.make_async_copy(cost.at[0, 0, span], cbuf.at[span], cost_sem.at[g])

    small = [
        pltpu.make_async_copy(src, dst, small_sem.at[k])
        for k, (src, dst) in enumerate((
            (rows_in, rows), (cols_in, cols), (tinit_in, init_pot), (slog_in, slog), (tlog_in, tlog),
        ))
    ]
    for copy in small:
        copy.start()
    for g in range(groups):
        fetch(g).start()

    total = count[0, 0]
    lane = lax.broadcasted_iota(jnp.int32, (LANES, LANES), 1)
    sub8 = lax.broadcasted_iota(jnp.int32, (GROUP, LANES), 0)
    slot = lax.broadcasted_iota(jnp.int32, (cap, LANES), 0)

    def segment(ids, s):
        return jnp.where(s < total, ids[0, 0, s], -1)

    def prepare(ids, seg, nb):
        def fill(g, _):
            value = jnp.zeros((GROUP, LANES), jnp.int32)
            for k in range(GROUP):
                value = jnp.where(sub8 == k, segment(ids, g * GROUP + k), value)
            seg[pl.ds(pl.multiple_of(g * GROUP, GROUP), GROUP), :] = value
            return 0

        lax.fori_loop(0, cap // GROUP, fill, 0)
        mine = seg[...]

        def earlier(g, dup):
            for k in range(GROUP):
                t = g * GROUP + k
                same = (mine == segment(ids, t)) & (slot > t)
                dup = jnp.where(same, 1.0, dup)
            return dup

        dup = jnp.zeros((cap, LANES), jnp.float32)
        dup = lax.fori_loop(0, cap // GROUP, earlier, dup)
        blocks = lax.broadcasted_iota(jnp.int32, (cap, nb), 1)
        one = jnp.where(mine[:, :nb] == blocks, 1.0, 0.0)
        return one, one * (1.0 - dup[:, :nb])

    def prepare_source():
        one, first = prepare(rows, seg_s, first_s.shape[1])
        first_s[...] = first
        one = one.astype(jnp.bfloat16)
        same = lax.dot_general(
            one, one, (((1,), (1,)), ((), ())), preferred_element_type=jnp.float32
        )
        same_s[...] = jnp.concatenate([same, same], axis=1).astype(jnp.bfloat16)

    def prepare_target():
        one, first = prepare(cols, seg_t, hot_t.shape[0])
        both = jnp.concatenate([one, first], axis=0).T
        one, first = both[:, :cap], both[:, cap:]
        hot_t[...] = jnp.concatenate([one, one], axis=1).astype(jnp.bfloat16)
        rep_t[...] = jnp.concatenate([first] * 4, axis=1).astype(jnp.bfloat16)

    def prepare_place(q, first):
        first = first.T
        place_s[q] = jnp.concatenate([first] * 4, axis=1).astype(jnp.bfloat16)
        found = jnp.sum(first, axis=1, keepdims=True)
        absent_s[q] = jnp.broadcast_to(jnp.where(found > 0.0, 0.0, -1e30), absent_s.shape[1:])

    gbuf[...] = jnp.zeros_like(gbuf)
    for copy in small:
        copy.wait()
    init_pot[...] = init_pot[...] * SCALE
    prepare_source()

    def gathered():
        pieces = [fine[pl.ds(k, cap, stride=GROUP), :] for k in range(GROUP)]
        lbuf[...] = join(pieces)

    def fine_row(s):
        return pl.ds(pl.multiple_of(s * GROUP, GROUP), GROUP)

    def first_pass():
        def group(g, _):
            base = g * TILES
            fetch(g).wait()
            for k in range(TILES):
                s = base + k
                tile = cbuf[s] * SCALE
                cbuf[s] = tile
                y = (tile - init_pot[pl.ds(cols[0, 0, s], 1), :]).T
                turned_cost[s] = y
                y = y.reshape(LANES // GROUP, GROUP, LANES)
                m = jnp.min(y, axis=0)
                t = jnp.sum(jnp.exp2(m[None] - y), axis=0)
                fine[fine_row(s), :] = jnp.log2(t) - m
            return 0

        lax.fori_loop(0, cap // TILES, group, 0)
        gathered()

    def lse_pass(pot, ids, tiles):
        def collect(g, _):
            for k in range(GROUP):
                s = g * GROUP + k
                gbuf[pl.ds(s, 1), :] = pot[pl.ds(ids[0, 0, s], 1), :]
            return 0

        lax.fori_loop(0, cap // GROUP, collect, 0)
        turned = gbuf[...].T
        for g in range(cap // WIDE):
            near[g] = turned if g == 0 else pltpu.roll(turned, LANES - g * WIDE, 1)

        def group(g, _):
            base = g * WIDE
            side = near[g]
            for k in range(WIDE):
                x = side[:, k : k + 1] - tiles[base + k]
                x = x.reshape(LANES // GROUP, GROUP, LANES)
                m = jnp.max(x, axis=0)
                t = jnp.sum(jnp.exp2(x - m[None]), axis=0)
                fine[fine_row(base + k), :] = m + jnp.log2(t)
            return 0

        lax.fori_loop(0, cap // WIDE, group, 0)
        gathered()

    def level(ids, seg):
        mine = seg[...]
        own = lbuf[...]

        def widen(g, best):
            for k in range(TILES):
                t = g * TILES + k
                other = jnp.maximum(best, lbuf[pl.ds(t, 1), :])
                best = jnp.where(mine == segment(ids, t), other, best)
            return best

        best = lax.fori_loop(0, cap // TILES, widen, own)
        return best, jnp.concatenate(split_bf16(jnp.exp2(own - best), 2), axis=0)

    def thirds(x):
        parts = split_bf16(x, 3)
        return jnp.concatenate(parts + [jnp.zeros_like(parts[0])], axis=0)

    def merge_source(slots):
        best, weight = level(rows, seg_s)
        mass = jnp.dot(same_s[...], weight, preferred_element_type=jnp.float32)
        slots[...] = best + jnp.log2(jnp.maximum(mass, 1.0))

    def merge_target(part):
        best, weight = level(cols, seg_t)
        mass = jnp.dot(hot_t[...], weight, preferred_element_type=jnp.float32)
        peak = jnp.dot(rep_t[...], thirds(best), preferred_element_type=jnp.float32)
        part[...] = jnp.where(mass > 0.0, peak + jnp.log2(mass), -1e30)

    pending = []

    def send_all(axis, src, inbox, send, recv):
        copies = []
        for o in range(1, sizes[axis]):
            copies.append(pltpu.make_async_remote_copy(
                src_ref=src,
                dst_ref=inbox.at[o - 1],
                send_sem=send.at[o - 1],
                recv_sem=recv.at[o - 1],
                device_id={axis: peer(axis, o)},
                device_id_type=MESH,
            ))
            copies[-1].start()
        pending.extend(copies)
        return copies

    def place(q, slots):
        spread = jnp.dot(place_s[q], thirds(slots), preferred_element_type=jnp.float32)
        return spread + absent_s[q]

    def exchange(axis, it, part, mid, pot, logmass, s_send, s_recv, g_send, g_recv):
        n = sizes[axis]
        chunk = part.shape[0] // n
        copies = []
        for o in range(1, n):
            to = peer(axis, o)
            copies.append(pltpu.make_async_remote_copy(
                src_ref=part.at[pl.ds(to * chunk, chunk)],
                dst_ref=mid.at[o - 1],
                send_sem=s_send.at[it, o - 1],
                recv_sem=s_recv.at[it, o - 1],
                device_id={axis: to},
                device_id_type=MESH,
            ))
            copies[-1].start()
        own = pl.ds(pl.multiple_of(me[axis] * chunk, chunk), chunk)
        parts = [part[own, :]]
        mass = logmass[own, :] * LOG2E
        for copy in copies:
            copy.wait_recv()
        parts += [mid[o] for o in range(n - 1)]
        pot[own, :] = mass - join(parts)
        pending.extend(copies)
        copies = []
        for o in range(1, n):
            copies.append(pltpu.make_async_remote_copy(
                src_ref=pot.at[own],
                dst_ref=pot.at[own],
                send_sem=g_send.at[it, o - 1],
                recv_sem=g_recv.at[it, o - 1],
                device_id={axis: peer(axis, o)},
                device_id_type=MESH,
            ))
            copies[-1].start()
        for copy in copies:
            copy.wait_recv()
        pending.extend(copies)

    pl.semaphore_wait(barrier, n_row + n_col - 2)
    firsts = send_all("col", first_s, first_in, first_send, first_recv)
    prepare_place(0, first_s[...])

    source = ((slots_s0, mid_s0, pot_s0), (slots_s1, mid_s1, pot_s1))
    target = ((part_t0, mid_t0, pot_t0), (part_t1, mid_t1, pot_t1))
    pot = init_pot
    for it in range(ITERS):
        slots, inbox, pot_s = source[it]
        if it == 0:
            first_pass()
        else:
            moved[...] = pot[...] - init_pot[...]
            lse_pass(moved, cols, turned_cost)
        merge_source(slots)
        copies = send_all("col", slots, inbox, slots_send.at[it], slots_recv.at[it])
        if it == 0:
            prepare_target()
            for q, copy in enumerate(firsts):
                copy.wait_recv()
                prepare_place(q + 1, first_in[q])
        parts = [place(0, slots[...])]
        for q, copy in enumerate(copies):
            copy.wait_recv()
            parts.append(place(q + 1, inbox[q]))
        pot_s[...] = slog[...] * LOG2E - join(parts)
        if it == ITERS - 1:
            s_out[...] = pot_s[...]
        part, mid, pot = target[it]
        lse_pass(pot_s, rows, cbuf)
        merge_target(part)
        exchange("row", it, part, mid, pot, tlog,
                 scatter_send_t, scatter_recv_t, gather_send_t, gather_recv_t)
    t_out[...] = pot[...]
    for copy in pending:
        copy.wait_send()


def local(
    n_row, n_col,
    cost_tiles, tile_rows, tile_cols, tile_count, source_logmass, target_logmass, target_init,
):
    cap, width = cost_tiles.shape[2], cost_tiles.shape[-1]
    nbs = source_logmass.shape[0] // width
    nbt = target_logmass.shape[0] // width
    f32, bf16 = jnp.float32, jnp.bfloat16
    vmem = pl.BlockSpec(memory_space=pltpu.VMEM)
    hbm = pl.BlockSpec(memory_space=pltpu.HBM)
    smem = pl.BlockSpec(memory_space=pltpu.SMEM)
    dma = pltpu.SemaphoreType.DMA
    scratch = [
        pltpu.SMEM((1, 1, cap), jnp.int32),
        pltpu.SMEM((1, 1, cap), jnp.int32),
        pltpu.VMEM((nbs, width), f32),
        pltpu.VMEM((nbt, width), f32),
        dma((5,)),
        pltpu.VMEM((cap, width, width), f32),
        pltpu.VMEM((cap, width, width), f32),
        pltpu.VMEM((cap * GROUP, width), f32),
        pltpu.VMEM((cap, width), f32),
        pltpu.VMEM((width, width), f32),
        pltpu.VMEM((cap // WIDE, width, width), f32),
        pltpu.VMEM((nbt, width), f32),
        pltpu.VMEM((nbt, width), f32),
        pltpu.VMEM((cap, width), jnp.int32),
        pltpu.VMEM((cap, width), jnp.int32),
        pltpu.VMEM((cap, 2 * cap), bf16),
        pltpu.VMEM((cap, nbs), f32),
        pltpu.VMEM((n_col - 1, cap, nbs), f32),
        pltpu.VMEM((n_col, nbs, 4 * cap), bf16),
        pltpu.VMEM((n_col, nbs, width), f32),
        pltpu.VMEM((nbt, 2 * cap), bf16),
        pltpu.VMEM((nbt, 4 * cap), bf16),
    ]
    scratch += [pltpu.VMEM((cap, width), f32)] * 2 + [pltpu.VMEM((nbt, width), f32)] * 2
    scratch += [pltpu.VMEM((n_col - 1, cap, width), f32)] * 2
    scratch += [pltpu.VMEM((n_row - 1, nbt // n_row, width), f32)] * 2
    scratch += [pltpu.VMEM((nbs, width), f32)] * 2 + [pltpu.VMEM((nbt, width), f32)] * 2
    scratch += [dma((cap // TILES,))]
    scratch += [dma((n_col - 1,))] * 2 + [dma((ITERS, n_col - 1))] * 2
    scratch += [dma((ITERS, n_row - 1))] * 4
    source, target = pl.pallas_call(
        functools.partial(kernel, n_row=n_row, n_col=n_col),
        out_shape=(
            pltpu.VMEM((nbs, width), f32),
            pltpu.VMEM((nbt, width), f32),
        ),
        in_specs=[hbm, hbm, hbm, smem, hbm, hbm, hbm],
        out_specs=(vmem, vmem),
        scratch_shapes=scratch,
        compiler_params=pltpu.CompilerParams(
            collective_id=0, has_side_effects=True, vmem_limit_bytes=64512 * 1024
        ),
        cost_estimate=pl.CostEstimate(
            flops=2 * ITERS * 5 * cap * width * width,
            bytes_accessed=4 * cap * width * width,
            transcendentals=2 * ITERS * cap * width * width,
        ),
    )(
        cost_tiles, tile_rows, tile_cols, tile_count,
        source_logmass.reshape(nbs, width),
        target_logmass.reshape(nbt, width),
        target_init.reshape(nbt, width),
    )
    return source.reshape(-1) / SCALE, target.reshape(-1) / SCALE


def solution(mesh):
    return jax.shard_map(
        functools.partial(local, mesh.shape["row"], mesh.shape["col"]),
        mesh=mesh,
        in_specs=(
            P("row", "col", None, None, None),
            P("row", "col", None),
            P("row", "col", None),
            P("row", "col"),
            P("row"),
            P("col"),
            P("col"),
        ),
        out_specs=(P("row"), P("col")),
        check_vma=False,
    )
```

```python
import functools
import math

import jax
import jax.numpy as jnp
from jax import lax
from jax.experimental import pallas as pl
from jax.experimental.pallas import tpu as pltpu
from jax.sharding import PartitionSpec as P

ITERS = 2
EPS = 0.1
LOG2E = math.log2(math.e)
SCALE = LOG2E / EPS
GROUP = 8
TILES = 16
WIDE = 32
LANES = 128
MESH = pl.DeviceIdType.MESH


def join(parts):
    top = functools.reduce(jnp.maximum, parts)
    total = functools.reduce(jnp.add, [jnp.exp2(p - top) for p in parts])
    return top + jnp.log2(total)


def split_bf16(x, parts):
    out = []
    for _ in range(parts):
        head = x.astype(jnp.bfloat16)
        out.append(head)
        x = x - head.astype(jnp.float32)
    return out


def kernel(
    cost, rows_in, cols_in, count, slog_in, tlog_in, tinit_in,
    s_out, t_out,
    rows, cols, slog, tlog, small_sem,
    cbuf, turned_cost, fine, lbuf, gbuf, moved, init_pot, seg_s, seg_t,
    same_s, first_s, first_in, place_s, absent_s, hot_t, rep_t,
    slots_s0, slots_s1, part_t0, part_t1,
    mid_s0, mid_s1, mid_t0, mid_t1,
    pot_s0, pot_s1, pot_t0, pot_t1,
    cost_sem, first_send, first_recv, slots_send, slots_recv,
    scatter_send_t, scatter_recv_t, gather_send_t, gather_recv_t,
    *, n_row, n_col,
):
    cap = cbuf.shape[0]
    me = {"row": lax.axis_index("row"), "col": lax.axis_index("col")}
    sizes = {"row": n_row, "col": n_col}

    def peer(axis, o):
        return lax.rem(me[axis] + o, sizes[axis])

    barrier = pltpu.get_barrier_semaphore()
    for axis in ("col", "row"):
        for o in range(1, sizes[axis]):
            pl.semaphore_signal(
                barrier, inc=1, device_id={axis: peer(axis, o)}, device_id_type=MESH
            )

    groups = cap // TILES

    def fetch(g):
        span = pl.ds(g * TILES, TILES)
        return pltpu.make_async_copy(cost.at[0, 0, span], cbuf.at[span], cost_sem.at[g])

    small = [
        pltpu.make_async_copy(src, dst, small_sem.at[k])
        for k, (src, dst) in enumerate((
            (rows_in, rows), (cols_in, cols), (tinit_in, init_pot), (slog_in, slog), (tlog_in, tlog),
        ))
    ]
    for copy in small:
        copy.start()
    for g in range(groups):
        fetch(g).start()

    total = count[0, 0]
    lane = lax.broadcasted_iota(jnp.int32, (LANES, LANES), 1)
    sub8 = lax.broadcasted_iota(jnp.int32, (GROUP, LANES), 0)
    slot = lax.broadcasted_iota(jnp.int32, (cap, LANES), 0)

    def segment(ids, s):
        return jnp.where(s < total, ids[0, 0, s], -1)

    def prepare(ids, seg, nb):
        def fill(g, _):
            value = jnp.zeros((GROUP, LANES), jnp.int32)
            for k in range(GROUP):
                value = jnp.where(sub8 == k, segment(ids, g * GROUP + k), value)
            seg[pl.ds(pl.multiple_of(g * GROUP, GROUP), GROUP), :] = value
            return 0

        lax.fori_loop(0, cap // GROUP, fill, 0)
        mine = seg[...]

        def earlier(g, dup):
            for k in range(GROUP):
                t = g * GROUP + k
                same = (mine == segment(ids, t)) & (slot > t)
                dup = jnp.where(same, 1.0, dup)
            return dup

        dup = jnp.zeros((cap, LANES), jnp.float32)
        dup = lax.fori_loop(0, cap // GROUP, earlier, dup)
        blocks = lax.broadcasted_iota(jnp.int32, (cap, nb), 1)
        one = jnp.where(mine[:, :nb] == blocks, 1.0, 0.0)
        return one, one * (1.0 - dup[:, :nb])

    def prepare_source():
        one, first = prepare(rows, seg_s, first_s.shape[1])
        first_s[...] = first
        one = one.astype(jnp.bfloat16)
        same = lax.dot_general(
            one, one, (((1,), (1,)), ((), ())), preferred_element_type=jnp.float32
        )
        same_s[...] = jnp.concatenate([same, same], axis=1).astype(jnp.bfloat16)

    def prepare_target():
        one, first = prepare(cols, seg_t, hot_t.shape[0])
        both = jnp.concatenate([one, first], axis=0).T
        one, first = both[:, :cap], both[:, cap:]
        hot_t[...] = jnp.concatenate([one, one], axis=1).astype(jnp.bfloat16)
        rep_t[...] = jnp.concatenate([first] * 4, axis=1).astype(jnp.bfloat16)

    def prepare_place(q, first):
        first = first.T
        place_s[q] = jnp.concatenate([first] * 4, axis=1).astype(jnp.bfloat16)
        found = jnp.sum(first, axis=1, keepdims=True)
        absent_s[q] = jnp.broadcast_to(jnp.where(found > 0.0, 0.0, -1e30), absent_s.shape[1:])

    gbuf[...] = jnp.zeros_like(gbuf)
    for copy in small:
        copy.wait()
    init_pot[...] = init_pot[...] * SCALE
    prepare_source()

    def gathered():
        pieces = [fine[pl.ds(k, cap, stride=GROUP), :] for k in range(GROUP)]
        lbuf[...] = join(pieces)

    def fine_row(s):
        return pl.ds(pl.multiple_of(s * GROUP, GROUP), GROUP)

    def first_pass():
        def group(g, _):
            base = g * WIDE
            for k in range(WIDE):
                s = base + k
                if k % TILES == 0:
                    fetch(g * (WIDE // TILES) + k // TILES).wait()
                tile = cbuf[s] * SCALE
                cbuf[s] = tile
                y = (tile - init_pot[pl.ds(cols[0, 0, s], 1), :]).T
                turned_cost[s] = y
                y = y.reshape(LANES // GROUP, GROUP, LANES)
                m = jnp.min(y, axis=0)
                t = jnp.sum(jnp.exp2(m[None] - y), axis=0)
                fine[fine_row(s), :] = jnp.log2(t) - m
            return 0

        lax.fori_loop(0, cap // WIDE, group, 0)
        gathered()

    def lse_pass(pot, ids, tiles):
        for s in range(cap):
            gbuf[s : s + 1, :] = pot[pl.ds(ids[0, 0, s], 1), :]
        side = gbuf[...].T
        for s in range(cap):
            x = side[:, s : s + 1] - tiles[s]
            x = x.reshape(LANES // GROUP, GROUP, LANES)
            m = jnp.max(x, axis=0)
            t = jnp.sum(jnp.exp2(x - m[None]), axis=0)
            fine[s * GROUP : (s + 1) * GROUP, :] = m + jnp.log2(t)
        gathered()

    def level(ids, seg):
        mine = seg[...]
        own = lbuf[...]

        def widen(g, best):
            for k in range(WIDE):
                t = g * WIDE + k
                other = jnp.maximum(best, lbuf[pl.ds(t, 1), :])
                best = jnp.where(mine == segment(ids, t), other, best)
            return best

        best = lax.fori_loop(0, cap // WIDE, widen, own)
        return best, jnp.concatenate(split_bf16(jnp.exp2(own - best), 2), axis=0)

    def thirds(x):
        parts = split_bf16(x, 3)
        return jnp.concatenate(parts + [jnp.zeros_like(parts[0])], axis=0)

    def merge_source(slots):
        best, weight = level(rows, seg_s)
        mass = jnp.dot(same_s[...], weight, preferred_element_type=jnp.float32)
        slots[...] = best + jnp.log2(jnp.maximum(mass, 1.0))

    def merge_target(part):
        best, weight = level(cols, seg_t)
        mass = jnp.dot(hot_t[...], weight, preferred_element_type=jnp.float32)
        peak = jnp.dot(rep_t[...], thirds(best), preferred_element_type=jnp.float32)
        part[...] = jnp.where(mass > 0.0, peak + jnp.log2(mass), -1e30)

    pending = []

    def send_all(axis, src, inbox, send, recv):
        copies = []
        for o in range(1, sizes[axis]):
            copies.append(pltpu.make_async_remote_copy(
                src_ref=src,
                dst_ref=inbox.at[o - 1],
                send_sem=send.at[o - 1],
                recv_sem=recv.at[o - 1],
                device_id={axis: peer(axis, o)},
                device_id_type=MESH,
            ))
            copies[-1].start()
        pending.extend(copies)
        return copies

    def place(q, slots):
        spread = jnp.dot(place_s[q], thirds(slots), preferred_element_type=jnp.float32)
        return spread + absent_s[q]

    def exchange(axis, it, part, mid, pot, logmass, s_send, s_recv, g_send, g_recv):
        n = sizes[axis]
        chunk = part.shape[0] // n
        copies = []
        for o in range(1, n):
            to = peer(axis, o)
            copies.append(pltpu.make_async_remote_copy(
                src_ref=part.at[pl.ds(to * chunk, chunk)],
                dst_ref=mid.at[o - 1],
                send_sem=s_send.at[it, o - 1],
                recv_sem=s_recv.at[it, o - 1],
                device_id={axis: to},
                device_id_type=MESH,
            ))
            copies[-1].start()
        own = pl.ds(pl.multiple_of(me[axis] * chunk, chunk), chunk)
        parts = [part[own, :]]
        mass = logmass[own, :] * LOG2E
        for copy in copies:
            copy.wait_recv()
        parts += [mid[o] for o in range(n - 1)]
        pot[own, :] = mass - join(parts)
        pending.extend(copies)
        copies = []
        for o in range(1, n):
            copies.append(pltpu.make_async_remote_copy(
                src_ref=pot.at[own],
                dst_ref=pot.at[own],
                send_sem=g_send.at[it, o - 1],
                recv_sem=g_recv.at[it, o - 1],
                device_id={axis: peer(axis, o)},
                device_id_type=MESH,
            ))
            copies[-1].start()
        for copy in copies:
            copy.wait_recv()
        pending.extend(copies)

    pl.semaphore_wait(barrier, n_row + n_col - 2)
    firsts = send_all("col", first_s, first_in, first_send, first_recv)
    prepare_place(0, first_s[...])

    source = ((slots_s0, mid_s0, pot_s0), (slots_s1, mid_s1, pot_s1))
    target = ((part_t0, mid_t0, pot_t0), (part_t1, mid_t1, pot_t1))
    pot = init_pot
    for it in range(ITERS):
        slots, inbox, pot_s = source[it]
        if it == 0:
            first_pass()
        else:
            moved[...] = pot[...] - init_pot[...]
            lse_pass(moved, cols, turned_cost)
        merge_source(slots)
        copies = send_all("col", slots, inbox, slots_send.at[it], slots_recv.at[it])
        if it == 0:
            prepare_target()
            for q, copy in enumerate(firsts):
                copy.wait_recv()
                prepare_place(q + 1, first_in[q])
        parts = [place(0, slots[...])]
        for q, copy in enumerate(copies):
            copy.wait_recv()
            parts.append(place(q + 1, inbox[q]))
        pot_s[...] = slog[...] * LOG2E - join(parts)
        if it == ITERS - 1:
            s_out[...] = pot_s[...]
        part, mid, pot = target[it]
        lse_pass(pot_s, rows, cbuf)
        merge_target(part)
        exchange("row", it, part, mid, pot, tlog,
                 scatter_send_t, scatter_recv_t, gather_send_t, gather_recv_t)
    t_out[...] = pot[...]
    for copy in pending:
        copy.wait_send()


def local(
    n_row, n_col,
    cost_tiles, tile_rows, tile_cols, tile_count, source_logmass, target_logmass, target_init,
):
    cap, width = cost_tiles.shape[2], cost_tiles.shape[-1]
    nbs = source_logmass.shape[0] // width
    nbt = target_logmass.shape[0] // width
    f32, bf16 = jnp.float32, jnp.bfloat16
    vmem = pl.BlockSpec(memory_space=pltpu.VMEM)
    hbm = pl.BlockSpec(memory_space=pltpu.HBM)
    smem = pl.BlockSpec(memory_space=pltpu.SMEM)
    dma = pltpu.SemaphoreType.DMA
    scratch = [
        pltpu.SMEM((1, 1, cap), jnp.int32),
        pltpu.SMEM((1, 1, cap), jnp.int32),
        pltpu.VMEM((nbs, width), f32),
        pltpu.VMEM((nbt, width), f32),
        dma((5,)),
        pltpu.VMEM((cap, width, width), f32),
        pltpu.VMEM((cap, width, width), f32),
        pltpu.VMEM((cap * GROUP, width), f32),
        pltpu.VMEM((cap, width), f32),
        pltpu.VMEM((width, width), f32),
        pltpu.VMEM((nbt, width), f32),
        pltpu.VMEM((nbt, width), f32),
        pltpu.VMEM((cap, width), jnp.int32),
        pltpu.VMEM((cap, width), jnp.int32),
        pltpu.VMEM((cap, 2 * cap), bf16),
        pltpu.VMEM((cap, nbs), f32),
        pltpu.VMEM((n_col - 1, cap, nbs), f32),
        pltpu.VMEM((n_col, nbs, 4 * cap), bf16),
        pltpu.VMEM((n_col, nbs, width), f32),
        pltpu.VMEM((nbt, 2 * cap), bf16),
        pltpu.VMEM((nbt, 4 * cap), bf16),
    ]
    scratch += [pltpu.VMEM((cap, width), f32)] * 2 + [pltpu.VMEM((nbt, width), f32)] * 2
    scratch += [pltpu.VMEM((n_col - 1, cap, width), f32)] * 2
    scratch += [pltpu.VMEM((n_row - 1, nbt // n_row, width), f32)] * 2
    scratch += [pltpu.VMEM((nbs, width), f32)] * 2 + [pltpu.VMEM((nbt, width), f32)] * 2
    scratch += [dma((cap // TILES,))]
    scratch += [dma((n_col - 1,))] * 2 + [dma((ITERS, n_col - 1))] * 2
    scratch += [dma((ITERS, n_row - 1))] * 4
    source, target = pl.pallas_call(
        functools.partial(kernel, n_row=n_row, n_col=n_col),
        out_shape=(
            pltpu.VMEM((nbs, width), f32),
            pltpu.VMEM((nbt, width), f32),
        ),
        in_specs=[hbm, hbm, hbm, smem, hbm, hbm, hbm],
        out_specs=(vmem, vmem),
        scratch_shapes=scratch,
        compiler_params=pltpu.CompilerParams(
            collective_id=0, has_side_effects=True, vmem_limit_bytes=64512 * 1024
        ),
        cost_estimate=pl.CostEstimate(
            flops=2 * ITERS * 5 * cap * width * width,
            bytes_accessed=4 * cap * width * width,
            transcendentals=2 * ITERS * cap * width * width,
        ),
    )(
        cost_tiles, tile_rows, tile_cols, tile_count,
        source_logmass.reshape(nbs, width),
        target_logmass.reshape(nbt, width),
        target_init.reshape(nbt, width),
    )
    return source.reshape(-1) / SCALE, target.reshape(-1) / SCALE


def solution(mesh):
    return jax.shard_map(
        functools.partial(local, mesh.shape["row"], mesh.shape["col"]),
        mesh=mesh,
        in_specs=(
            P("row", "col", None, None, None),
            P("row", "col", None),
            P("row", "col", None),
            P("row", "col"),
            P("row"),
            P("col"),
            P("col"),
        ),
        out_specs=(P("row"), P("col")),
        check_vma=False,
    )
```

```python
import functools
import math

import jax
import jax.numpy as jnp
from jax import lax
from jax.experimental import pallas as pl
from jax.experimental.pallas import tpu as pltpu
from jax.sharding import PartitionSpec as P

ITERS = 2
EPS = 0.1
LOG2E = math.log2(math.e)
SCALE = LOG2E / EPS
GROUP = 8
TILES = 16
WIDE = 32
LANES = 128
MESH = pl.DeviceIdType.MESH


def join(parts):
    top = functools.reduce(jnp.maximum, parts)
    total = functools.reduce(jnp.add, [jnp.exp2(p - top) for p in parts])
    return top + jnp.log2(total)


def split_bf16(x, parts):
    out = []
    for _ in range(parts):
        head = x.astype(jnp.bfloat16)
        out.append(head)
        x = x - head.astype(jnp.float32)
    return out


def kernel(
    cost, rows_in, cols_in, count, slog_in, tlog_in, tinit_in,
    s_out, t_out,
    rows, cols, slog, tlog, small_sem,
    cbuf, turned_cost, fine, lbuf, gbuf, moved, init_pot, seg_s, seg_t,
    same_s, first_s, first_in, place_s, absent_s, hot_t, rep_t,
    slots_s0, slots_s1, part_t0, part_t1,
    mid_s0, mid_s1, mid_t0, mid_t1,
    pot_s0, pot_s1, pot_t0, pot_t1,
    cost_sem, first_send, first_recv, slots_send, slots_recv,
    scatter_send_t, scatter_recv_t, gather_send_t, gather_recv_t,
    *, n_row, n_col,
):
    cap = cbuf.shape[0]
    me = {"row": lax.axis_index("row"), "col": lax.axis_index("col")}
    sizes = {"row": n_row, "col": n_col}

    def peer(axis, o):
        return lax.rem(me[axis] + o, sizes[axis])

    barrier = pltpu.get_barrier_semaphore()
    for axis in ("col", "row"):
        for o in range(1, sizes[axis]):
            pl.semaphore_signal(
                barrier, inc=1, device_id={axis: peer(axis, o)}, device_id_type=MESH
            )

    groups = cap // TILES

    def fetch(g):
        span = pl.ds(g * TILES, TILES)
        return pltpu.make_async_copy(cost.at[0, 0, span], cbuf.at[span], cost_sem.at[g])

    small = [
        pltpu.make_async_copy(src, dst, small_sem.at[k])
        for k, (src, dst) in enumerate((
            (rows_in, rows), (cols_in, cols), (tinit_in, init_pot), (slog_in, slog), (tlog_in, tlog),
        ))
    ]
    for copy in small:
        copy.start()
    for g in range(groups):
        fetch(g).start()

    total = count[0, 0]
    sub8 = lax.broadcasted_iota(jnp.int32, (GROUP, LANES), 0)

    def segment(ids, s):
        return jnp.where(s < total, ids[0, 0, s], -1)

    def prepare(ids, seg, nb):
        def fill(g, _):
            value = jnp.zeros((GROUP, LANES), jnp.int32)
            for k in range(GROUP):
                value = jnp.where(sub8 == k, segment(ids, g * GROUP + k), value)
            seg[pl.ds(pl.multiple_of(g * GROUP, GROUP), GROUP), :] = value
            return 0

        lax.fori_loop(0, cap // GROUP, fill, 0)
        mine = seg[...]

        blocks = lax.broadcasted_iota(jnp.int32, (cap, nb), 1)
        one = jnp.where(mine[:, :nb] == blocks, 1.0, 0.0)
        half = one.astype(jnp.bfloat16)
        same = lax.dot_general(
            half, half, (((1,), (1,)), ((), ())), preferred_element_type=jnp.float32
        )
        across = lax.broadcasted_iota(jnp.int32, (cap, cap), 1)
        down = lax.broadcasted_iota(jnp.int32, (cap, cap), 0)
        before = jnp.sum(jnp.where(across < down, same, 0.0), axis=1, keepdims=True)
        return one, jnp.where(before > 0.0, 0.0, one), same

    def prepare_source():
        _, first, same = prepare(rows, seg_s, first_s.shape[1])
        first_s[...] = first
        same_s[...] = jnp.concatenate([same, same], axis=1).astype(jnp.bfloat16)

    def prepare_target():
        one, first, _ = prepare(cols, seg_t, hot_t.shape[0])
        both = jnp.concatenate([one, first], axis=0).T
        one, first = both[:, :cap], both[:, cap:]
        hot_t[...] = jnp.concatenate([one, one], axis=1).astype(jnp.bfloat16)
        rep_t[...] = jnp.concatenate([first] * 4, axis=1).astype(jnp.bfloat16)

    def prepare_place(q, first):
        first = first.T
        place_s[q] = jnp.concatenate([first] * 4, axis=1).astype(jnp.bfloat16)
        found = jnp.sum(first, axis=1, keepdims=True)
        absent_s[q] = jnp.broadcast_to(jnp.where(found > 0.0, 0.0, -1e30), absent_s.shape[1:])

    gbuf[...] = jnp.zeros_like(gbuf)
    for copy in small:
        copy.wait()
    init_pot[...] = init_pot[...] * SCALE
    prepare_source()

    def gathered():
        pieces = [fine[pl.ds(k, cap, stride=GROUP), :] for k in range(GROUP)]
        lbuf[...] = join(pieces)

    def fine_row(s):
        return pl.ds(pl.multiple_of(s * GROUP, GROUP), GROUP)

    def first_pass():
        def group(g, _):
            base = g * WIDE
            for k in range(WIDE):
                s = base + k
                if k % TILES == 0:
                    fetch(g * (WIDE // TILES) + k // TILES).wait()
                tile = cbuf[s] * SCALE
                cbuf[s] = tile
                y = (tile - init_pot[pl.ds(cols[0, 0, s], 1), :]).T
                turned_cost[s] = y
                y = y.reshape(LANES // GROUP, GROUP, LANES)
                m = jnp.min(y, axis=0)
                t = jnp.sum(jnp.exp2(m[None] - y), axis=0)
                fine[fine_row(s), :] = jnp.log2(t) - m
            return 0

        lax.fori_loop(0, cap // WIDE, group, 0)
        gathered()

    def lse_pass(pot, ids, tiles):
        for s in range(cap):
            gbuf[s : s + 1, :] = pot[pl.ds(ids[0, 0, s], 1), :]
        side = gbuf[...].T
        for s in range(cap):
            x = side[:, s : s + 1] - tiles[s]
            x = x.reshape(LANES // GROUP, GROUP, LANES)
            m = jnp.max(x, axis=0)
            t = jnp.sum(jnp.exp2(x - m[None]), axis=0)
            fine[s * GROUP : (s + 1) * GROUP, :] = m + jnp.log2(t)
        gathered()

    def level(ids, seg):
        mine = seg[...]
        own = lbuf[...]

        def widen(g, best):
            for k in range(WIDE):
                t = g * WIDE + k
                other = jnp.maximum(best, lbuf[pl.ds(t, 1), :])
                best = jnp.where(mine == segment(ids, t), other, best)
            return best

        best = lax.fori_loop(0, cap // WIDE, widen, own)
        return best, jnp.concatenate(split_bf16(jnp.exp2(own - best), 2), axis=0)

    def thirds(x):
        parts = split_bf16(x, 3)
        return jnp.concatenate(parts + [jnp.zeros_like(parts[0])], axis=0)

    def merge_source(slots):
        best, weight = level(rows, seg_s)
        mass = jnp.dot(same_s[...], weight, preferred_element_type=jnp.float32)
        slots[...] = best + jnp.log2(jnp.maximum(mass, 1.0))

    def merge_target(part):
        best, weight = level(cols, seg_t)
        mass = jnp.dot(hot_t[...], weight, preferred_element_type=jnp.float32)
        peak = jnp.dot(rep_t[...], thirds(best), preferred_element_type=jnp.float32)
        part[...] = jnp.where(mass > 0.0, peak + jnp.log2(mass), -1e30)

    pending = []

    def send_all(axis, src, inbox, send, recv):
        copies = []
        for o in range(1, sizes[axis]):
            copies.append(pltpu.make_async_remote_copy(
                src_ref=src,
                dst_ref=inbox.at[o - 1],
                send_sem=send.at[o - 1],
                recv_sem=recv.at[o - 1],
                device_id={axis: peer(axis, o)},
                device_id_type=MESH,
            ))
            copies[-1].start()
        pending.extend(copies)
        return copies

    def place(q, slots):
        spread = jnp.dot(place_s[q], thirds(slots), preferred_element_type=jnp.float32)
        return spread + absent_s[q]

    def exchange(axis, it, part, mid, pot, logmass, s_send, s_recv, g_send, g_recv):
        n = sizes[axis]
        chunk = part.shape[0] // n
        copies = []
        for o in range(1, n):
            to = peer(axis, o)
            copies.append(pltpu.make_async_remote_copy(
                src_ref=part.at[pl.ds(to * chunk, chunk)],
                dst_ref=mid.at[o - 1],
                send_sem=s_send.at[it, o - 1],
                recv_sem=s_recv.at[it, o - 1],
                device_id={axis: to},
                device_id_type=MESH,
            ))
            copies[-1].start()
        own = pl.ds(pl.multiple_of(me[axis] * chunk, chunk), chunk)
        parts = [part[own, :]]
        mass = logmass[own, :] * LOG2E
        for copy in copies:
            copy.wait_recv()
        parts += [mid[o] for o in range(n - 1)]
        pot[own, :] = mass - join(parts)
        pending.extend(copies)
        copies = []
        for o in range(1, n):
            copies.append(pltpu.make_async_remote_copy(
                src_ref=pot.at[own],
                dst_ref=pot.at[own],
                send_sem=g_send.at[it, o - 1],
                recv_sem=g_recv.at[it, o - 1],
                device_id={axis: peer(axis, o)},
                device_id_type=MESH,
            ))
            copies[-1].start()
        for copy in copies:
            copy.wait_recv()
        pending.extend(copies)

    pl.semaphore_wait(barrier, n_row + n_col - 2)
    firsts = send_all("col", first_s, first_in, first_send, first_recv)
    prepare_place(0, first_s[...])

    source = ((slots_s0, mid_s0, pot_s0), (slots_s1, mid_s1, pot_s1))
    target = ((part_t0, mid_t0, pot_t0), (part_t1, mid_t1, pot_t1))
    pot = init_pot
    for it in range(ITERS):
        slots, inbox, pot_s = source[it]
        if it == 0:
            first_pass()
        else:
            moved[...] = pot[...] - init_pot[...]
            lse_pass(moved, cols, turned_cost)
        merge_source(slots)
        copies = send_all("col", slots, inbox, slots_send.at[it], slots_recv.at[it])
        if it == 0:
            prepare_target()
            for q, copy in enumerate(firsts):
                copy.wait_recv()
                prepare_place(q + 1, first_in[q])
        parts = [place(0, slots[...])]
        for q, copy in enumerate(copies):
            copy.wait_recv()
            parts.append(place(q + 1, inbox[q]))
        pot_s[...] = slog[...] * LOG2E - join(parts)
        if it == ITERS - 1:
            s_out[...] = pot_s[...]
        part, mid, pot = target[it]
        lse_pass(pot_s, rows, cbuf)
        merge_target(part)
        exchange("row", it, part, mid, pot, tlog,
                 scatter_send_t, scatter_recv_t, gather_send_t, gather_recv_t)
    t_out[...] = pot[...]
    for copy in pending:
        copy.wait_send()


def local(
    n_row, n_col,
    cost_tiles, tile_rows, tile_cols, tile_count, source_logmass, target_logmass, target_init,
):
    cap, width = cost_tiles.shape[2], cost_tiles.shape[-1]
    nbs = source_logmass.shape[0] // width
    nbt = target_logmass.shape[0] // width
    f32, bf16 = jnp.float32, jnp.bfloat16
    vmem = pl.BlockSpec(memory_space=pltpu.VMEM)
    hbm = pl.BlockSpec(memory_space=pltpu.HBM)
    smem = pl.BlockSpec(memory_space=pltpu.SMEM)
    dma = pltpu.SemaphoreType.DMA
    scratch = [
        pltpu.SMEM((1, 1, cap), jnp.int32),
        pltpu.SMEM((1, 1, cap), jnp.int32),
        pltpu.VMEM((nbs, width), f32),
        pltpu.VMEM((nbt, width), f32),
        dma((5,)),
        pltpu.VMEM((cap, width, width), f32),
        pltpu.VMEM((cap, width, width), f32),
        pltpu.VMEM((cap * GROUP, width), f32),
        pltpu.VMEM((cap, width), f32),
        pltpu.VMEM((width, width), f32),
        pltpu.VMEM((nbt, width), f32),
        pltpu.VMEM((nbt, width), f32),
        pltpu.VMEM((cap, width), jnp.int32),
        pltpu.VMEM((cap, width), jnp.int32),
        pltpu.VMEM((cap, 2 * cap), bf16),
        pltpu.VMEM((cap, nbs), f32),
        pltpu.VMEM((n_col - 1, cap, nbs), f32),
        pltpu.VMEM((n_col, nbs, 4 * cap), bf16),
        pltpu.VMEM((n_col, nbs, width), f32),
        pltpu.VMEM((nbt, 2 * cap), bf16),
        pltpu.VMEM((nbt, 4 * cap), bf16),
    ]
    scratch += [pltpu.VMEM((cap, width), f32)] * 2 + [pltpu.VMEM((nbt, width), f32)] * 2
    scratch += [pltpu.VMEM((n_col - 1, cap, width), f32)] * 2
    scratch += [pltpu.VMEM((n_row - 1, nbt // n_row, width), f32)] * 2
    scratch += [pltpu.VMEM((nbs, width), f32)] * 2 + [pltpu.VMEM((nbt, width), f32)] * 2
    scratch += [dma((cap // TILES,))]
    scratch += [dma((n_col - 1,))] * 2 + [dma((ITERS, n_col - 1))] * 2
    scratch += [dma((ITERS, n_row - 1))] * 4
    source, target = pl.pallas_call(
        functools.partial(kernel, n_row=n_row, n_col=n_col),
        out_shape=(
            pltpu.VMEM((nbs, width), f32),
            pltpu.VMEM((nbt, width), f32),
        ),
        in_specs=[hbm, hbm, hbm, smem, hbm, hbm, hbm],
        out_specs=(vmem, vmem),
        scratch_shapes=scratch,
        compiler_params=pltpu.CompilerParams(
            collective_id=0, has_side_effects=True, vmem_limit_bytes=64512 * 1024
        ),
        cost_estimate=pl.CostEstimate(
            flops=2 * ITERS * 5 * cap * width * width,
            bytes_accessed=4 * cap * width * width,
            transcendentals=2 * ITERS * cap * width * width,
        ),
    )(
        cost_tiles, tile_rows, tile_cols, tile_count,
        source_logmass.reshape(nbs, width),
        target_logmass.reshape(nbt, width),
        target_init.reshape(nbt, width),
    )
    return source.reshape(-1) / SCALE, target.reshape(-1) / SCALE


def solution(mesh):
    return jax.shard_map(
        functools.partial(local, mesh.shape["row"], mesh.shape["col"]),
        mesh=mesh,
        in_specs=(
            P("row", "col", None, None, None),
            P("row", "col", None),
            P("row", "col", None),
            P("row", "col"),
            P("row"),
            P("col"),
            P("col"),
        ),
        out_specs=(P("row"), P("col")),
        check_vma=False,
    )
```
